256 devices in a mesh: ctx: 32 (over x_lo, z, core), tp: 8 (over x_hi, y).
Axes of the slice: x: 4 (x_hi: 2, x_lo: 2; x = x_hi * 2 + x_lo), y: 4, z: 8, core: 2. Of those that a mesh axis runs over, the one named last changes fastest.
Arguments:
- queries: bfloat16 [4096, 3072], P('ctx', 'tp'), may hold values from -5 to 5
- key_rows: bfloat16 [4096, 1024], P('ctx', 'tp'), may hold values from -5 to 5
- value_rows: bfloat16 [4096, 1024], P('ctx', 'tp'), may hold values from -6 to 6
- attn_out: bfloat16 [4096, 3072], P('ctx', 'tp'), may hold values from -6 to 6
- grad_out: bfloat16 [4096, 3072], P('ctx', 'tp'), may hold values from -16 to 16
- segments: int32 [4096], replicated, may hold values from 0 to 2, never falling along the last dimension, each value on 1 to 2560 neighbouring positions
- grad_moe_out: bfloat16 [4096, 3072], P('ctx'), may hold values from -12 to 12
- expert_ids: int32 [4096, 2], P('ctx'), may hold values from 0 to 7, as said below
- route_weights: float32 [4096, 2], P('ctx'), may hold values from 0.2 to 1
- saved_gate: bfloat16 [36864, 4096], P('ctx', 'tp'), may hold values from -6 to 6
- saved_up: bfloat16 [36864, 4096], P('ctx', 'tp'), may hold values from -6 to 6
- w_gate: bfloat16 [3072, 131072], P(None, ('ctx', 'tp')), may hold values from -0.109375 to 0.109375
- w_up: bfloat16 [3072, 131072], P(None, ('ctx', 'tp')), may hold values from -0.109375 to 0.109375
- w_down: bfloat16 [131072, 3072], P(('ctx', 'tp')), may hold values from -0.046875 to 0.046875
Outputs:
- grad_queries: bfloat16 [4096, 3072], P('ctx', 'tp')
- grad_keys: bfloat16 [4096, 1024], P('ctx', 'tp')
- grad_values: bfloat16 [4096, 1024], P('ctx', 'tp')
- grad_moe_in: bfloat16 [4096, 3072], P('ctx', 'tp')
The draws below stay inside these ranges and needn't reach their ends.
Inputs may be any that keep to these rules, and one draw needn't show every extreme that they name: `expert_ids`: A token's two ids differ. In each aligned block of 128 tokens no expert is named more than 36 times, and one expert, the same in every block, is named exactly 36 times in each block.
All inputs are finite; a program needn't handle non-finite values.
Results may differ from the reference program's by a relative error of at most 0.02.
Values may be sent and summed in bfloat16 or wider, within the bound.
A program may use at most 128 MiB of HBM per device.

```python
import math
import jax
import jax.numpy as jnp
import numpy as np
from jax import lax

D = 3072
FF = 16384
EXPERTS = 8
QH = 24
KVH = 8
HEAD = 128
CT = 128
SEQ = 4096
CAP = 36
HID = 512
N_CTX = 32
N_TP = 8
DEVICES = 256


def draw_queries(key, part):
    key = jax.random.fold_in(key, 3)
    values_drawn = jnp.clip(jax.random.normal(key, (SEQ, QH * HEAD), jnp.float32), -5.0, 5.0)
    return values_drawn.astype(jnp.bfloat16)


def draw_key_rows(key, part):
    key = jax.random.fold_in(key, 5)
    values_drawn = jnp.clip(jax.random.normal(key, (SEQ, KVH * HEAD), jnp.float32), -5.0, 5.0)
    return values_drawn.astype(jnp.bfloat16)


def draw_expert_ids(key, part):
    key = jax.random.fold_in(key, 7)
    hot_expert = jax.random.randint(jax.random.fold_in(key, 1), (), 0, EXPERTS)
    block_keys = jax.random.split(jax.random.fold_in(key, 2), N_CTX)
    remaining = 2 * CT - CAP
    even_load = remaining // (EXPERTS - 1)
    leftover = remaining - even_load * (EXPERTS - 1)
    margin = max(CAP - even_load - 1, 0)
    pair_count = (EXPERTS - 1) // 2

    def one_block(block_key):
        order_key, shift_key, token_key, flip_key = jax.random.split(block_key, 4)
        others = jax.random.permutation(order_key, EXPERTS - 1)
        other_loads = even_load + (others < leftover).astype(jnp.int32)
        shifts = jax.random.randint(shift_key, (pair_count,), 0, margin + 1)
        load_moves = jnp.concatenate([jnp.stack([shifts, -shifts], axis=1).reshape(-1), jnp.zeros((EXPERTS - 1 - 2 * pair_count,), jnp.int32)])
        other_loads = other_loads + load_moves
        expert_index = jnp.arange(EXPERTS, dtype=jnp.int32)
        other_index = jnp.clip(expert_index - (expert_index > hot_expert).astype(jnp.int32), 0, EXPERTS - 2)
        expert_loads = jnp.where(expert_index == hot_expert, CAP, other_loads[other_index])
        bounds = jnp.cumsum(expert_loads)
        positions = jnp.arange(2 * CT, dtype=jnp.int32)
        labels = jnp.sum((positions[:, None] >= bounds[None, :]).astype(jnp.int32), axis=1)
        token_order = jax.random.permutation(token_key, CT)
        first_id = labels[token_order]
        second_id = labels[token_order + CT]
        swapped = jax.random.randint(flip_key, (CT,), 0, 2) == 1
        return jnp.stack([jnp.where(swapped, second_id, first_id), jnp.where(swapped, first_id, second_id)], axis=1)
    return jax.vmap(one_block)(block_keys).reshape(N_CTX * CT, 2).astype(jnp.int32)


def steps_of(own_key, shape, pieces, smallest, high):
    level, own = 1.0, jax.random.fold_in(own_key, 6)
    for dim, blocks in pieces:
        draws = jnp.exp(jax.random.uniform(jax.random.fold_in(own, dim), (blocks,), jnp.float32, smallest / len(pieces), high / len(pieces)))
        level = level * jnp.repeat(draws, shape[dim] // blocks).reshape([-1 if axis == dim else 1 for axis in range(len(shape))])
    return level


def length_profile(number_of, total, most, slope):
    weights = [(1 << 20) // math.isqrt(rank ** slope) + 1 for rank in range(2, number_of + 1)]
    surplus, counts = total - most - (number_of - 1), [1] * (number_of - 1)
    while surplus > 0:
        free = [i for i in range(number_of - 1) if counts[i] < most]
        pool, left = sum([weights[i] for i in free]), surplus
        for i in free:
            addition = min(most - counts[i], max(1, left * weights[i] // pool), surplus)
            counts[i] = counts[i] + addition
            surplus = surplus - addition
    return np.array([most] + counts)


def ragged(stream_key, count, total, limit, lean):
    if count == 2:
        one = jax.random.randint(stream_key, (), max(1, total - limit), min(limit, total - 1) + 1)
        return jnp.stack([one, total - one])
    tallies = jnp.asarray(length_profile(count, total, limit, lean), jnp.int32)
    couples = (count - 1) // 2
    source_of, sink = tallies[1:1 + 2 * couples:2], tallies[2:2 + 2 * couples:2]
    slack = jnp.minimum(source_of - 1, limit - sink)
    passed = jax.random.randint(jax.random.fold_in(stream_key, 1), (couples,), 0, 1 << 20) % (slack + 1)
    tallies = tallies.at[1:1 + 2 * couples:2].set(source_of - passed).at[2:2 + 2 * couples:2].set(sink + passed)
    return tallies[jax.random.permutation(jax.random.fold_in(stream_key, 2), count)]


def gaussian(own_key, dims, spread, reach, pieces=(), held_as=jnp.bfloat16):
    result = jax.random.normal(own_key, dims, jnp.float32) * spread
    if len(pieces) > 0:
        result = steps_of(own_key, dims, pieces, -0.22, 0.18) * result
    return jnp.clip(result, min=-reach, max=reach).astype(held_as)


def setup_inputs(seed: int = 0) -> dict:
    seeds = jax.random.split(jax.random.key(seed), 15)
    return {
        "queries": draw_queries(jax.random.fold_in(seeds[14], 71), 0),
        "key_rows": draw_key_rows(jax.random.fold_in(seeds[14], 71), 0),
        "value_rows": gaussian(seeds[2], (SEQ, KVH * HEAD), 1.0, 6.0, ((0, 32), (1, 8))),
        "attn_out": gaussian(seeds[3], (SEQ, QH * HEAD), 1.0, 6.0, ((0, 32), (1, 8))),
        "grad_out": gaussian(seeds[4], (SEQ, QH * HEAD), 4.0, 16.0, ((0, 32), (1, 8))),
        "segments": jnp.searchsorted(jnp.cumsum(ragged(seeds[5], 3, SEQ, 5 * SEQ // 8, 0)), jnp.arange(SEQ), side="right").astype(jnp.int32),
        "grad_moe_out": gaussian(seeds[6], (SEQ, D), 2.0, 12.0, ((0, 32),)),
        "expert_ids": draw_expert_ids(jax.random.fold_in(seeds[14], 71), 0),
        "route_weights": jnp.clip(0.2 + 0.8 * jax.random.uniform(seeds[8], (SEQ, 2), jnp.float32) ** steps_of(seeds[8], (SEQ, 2), ((0, 32),), -0.2, 0.2), 0.2, 1.0),
        "saved_gate": gaussian(seeds[9], (N_CTX * N_CTX * CAP, HID * N_TP), 1.0, 6.0, ((0, 32), (1, 8))),
        "saved_up": gaussian(seeds[10], (N_CTX * N_CTX * CAP, HID * N_TP), 1.0, 6.0, ((0, 32), (1, 8))),
        "w_gate": gaussian(seeds[11], (D, EXPERTS * FF), D ** -0.5, 0.109375, ((1, 256),)),
        "w_up": gaussian(seeds[12], (D, EXPERTS * FF), D ** -0.5, 0.109375, ((1, 256),)),
        "w_down": gaussian(seeds[13], (EXPERTS * FF, D), FF ** -0.5, 0.046875, ((0, 256),)),
    }


def reference(queries, key_rows, value_rows, attn_out, grad_out, segments, grad_moe_out, expert_ids, route_weights, saved_gate, saved_up, w_gate, w_up, w_down):
    group_size = QH // KVH
    scaling = HEAD ** -0.5
    block_size = min(512, SEQ)
    block_count = SEQ // block_size
    positions = jnp.arange(SEQ, dtype=jnp.int32)

    def per_head(inputs):
        query_head, key_head, value_head, grad_head, out_head = inputs
        key_float = key_head.astype(jnp.float32)
        value_float = value_head.astype(jnp.float32)

        def query_step(running, block_index):
            key_sum, value_sum = running
            first_row = (block_index * block_size).astype(jnp.int32)
            query_part = lax.dynamic_slice_in_dim(query_head, first_row, block_size, 0).astype(jnp.float32)
            grad_part = lax.dynamic_slice_in_dim(grad_head, first_row, block_size, 0).astype(jnp.float32)
            out_part = lax.dynamic_slice_in_dim(out_head, first_row, block_size, 0).astype(jnp.float32)
            query_pos = first_row + jnp.arange(block_size, dtype=jnp.int32)
            query_seg = lax.dynamic_slice_in_dim(segments, first_row, block_size, 0)
            visible = (positions[None, :] <= query_pos[:, None]) & (segments[None, :] == query_seg[:, None])
            scores = scaling * jnp.einsum("qgd,kd->gqk", query_part, key_float)
            highest = jnp.max(jnp.where(visible[None], scores, -1e30), axis=-1, keepdims=True)
            denominator = jnp.sum(jnp.where(visible[None], jnp.exp(scores - highest), 0.0), axis=-1, keepdims=True)
            logsum = highest + jnp.log(denominator)
            soft_weights = jnp.where(visible[None], jnp.exp(scores - logsum), 0.0)
            row_dots = jnp.einsum("qgd,qgd->gq", grad_part, out_part)
            grad_probs = jnp.einsum("qgd,kd->gqk", grad_part, value_float)
            grad_scores = lax.optimization_barrier((soft_weights * (grad_probs - row_dots[..., None])).astype(jnp.bfloat16)).astype(jnp.float32)
            probs_low = lax.optimization_barrier(soft_weights.astype(jnp.bfloat16)).astype(jnp.float32)
            grad_query = scaling * jnp.einsum("gqk,kd->qgd", grad_scores, key_float)
            key_sum = key_sum + scaling * jnp.einsum("gqk,qgd->kd", grad_scores, query_part)
            value_sum = value_sum + jnp.einsum("gqk,qgd->kd", probs_low, grad_part)
            return (key_sum, value_sum), grad_query.astype(jnp.bfloat16)

        start_sums = (jnp.zeros((SEQ, HEAD), jnp.float32), jnp.zeros((SEQ, HEAD), jnp.float32))
        (key_sum, value_sum), grad_blocks = lax.scan(query_step, start_sums, jnp.arange(block_count, dtype=jnp.int32))
        return grad_blocks.reshape(SEQ, group_size, HEAD), key_sum.astype(jnp.bfloat16), value_sum.astype(jnp.bfloat16)

    query_heads = queries.reshape(SEQ, KVH, group_size, HEAD).transpose(1, 0, 2, 3)
    grad_heads = grad_out.reshape(SEQ, KVH, group_size, HEAD).transpose(1, 0, 2, 3)
    out_heads = attn_out.reshape(SEQ, KVH, group_size, HEAD).transpose(1, 0, 2, 3)
    key_heads = key_rows.reshape(SEQ, KVH, HEAD).transpose(1, 0, 2)
    value_heads = value_rows.reshape(SEQ, KVH, HEAD).transpose(1, 0, 2)
    grad_query_all, grad_key_all, grad_value_all = lax.map(per_head, (query_heads, key_heads, value_heads, grad_heads, out_heads))
    grad_queries = grad_query_all.transpose(1, 0, 2, 3).reshape(SEQ, QH * HEAD)
    grad_keys = grad_key_all.transpose(1, 0, 2).reshape(SEQ, KVH * HEAD)
    grad_values = grad_value_all.transpose(1, 0, 2).reshape(SEQ, KVH * HEAD)

    copies = N_CTX // EXPERTS
    slot_total = N_CTX * CAP
    pair_ids = expert_ids.reshape(N_CTX, 2 * CT).astype(jnp.int32)
    onehot = (pair_ids[..., None] == jnp.arange(EXPERTS, dtype=jnp.int32)).astype(jnp.int32)
    earlier = (jnp.cumsum(onehot, axis=1) - onehot).astype(jnp.int32)
    slot_rank = jnp.sum(earlier * onehot, axis=-1).astype(jnp.int32)
    source = jnp.arange(N_CTX, dtype=jnp.int32)[:, None]
    slot_row = (source * CAP + slot_rank).astype(jnp.int32)
    token_of = (source * CT + jnp.arange(2 * CT, dtype=jnp.int32)[None, :] // 2).astype(jnp.int32)
    dispatched = jnp.zeros((EXPERTS, slot_total, D), jnp.bfloat16).at[pair_ids, slot_row].set(grad_moe_out[token_of])

    def slice_term(slice_index, returned):
        slice_index = jnp.asarray(slice_index).astype(jnp.int32)
        column = slice_index // N_TP
        tp_pos = slice_index % N_TP
        expert = column // copies
        row_data = lax.dynamic_index_in_dim(dispatched, expert, 0, keepdims=False)
        gate_pre = lax.dynamic_slice(saved_gate, (column * slot_total, tp_pos * HID), (slot_total, HID)).astype(jnp.float32)
        up_pre = lax.dynamic_slice(saved_up, (column * slot_total, tp_pos * HID), (slot_total, HID)).astype(jnp.float32)
        gate_cols = lax.dynamic_slice_in_dim(w_gate, slice_index * HID, HID, 1)
        up_cols = lax.dynamic_slice_in_dim(w_up, slice_index * HID, HID, 1)
        down_rows = lax.dynamic_slice_in_dim(w_down, slice_index * HID, HID, 0)
        hidden_grad = jnp.dot(row_data, down_rows.T, preferred_element_type=jnp.float32)
        sigmoid_gate = jax.nn.sigmoid(gate_pre)
        grad_up = (hidden_grad * gate_pre * sigmoid_gate).astype(jnp.bfloat16)
        grad_gate = (hidden_grad * up_pre * sigmoid_gate * (1.0 + gate_pre * (1.0 - sigmoid_gate))).astype(jnp.bfloat16)
        partial_rows = jnp.dot(grad_gate, gate_cols.T, preferred_element_type=jnp.float32) + jnp.dot(grad_up, up_cols.T, preferred_element_type=jnp.float32)
        rounded = lax.optimization_barrier(partial_rows.astype(jnp.bfloat16)).astype(jnp.float32)
        current = lax.dynamic_index_in_dim(returned, expert, 0, keepdims=False)
        return lax.dynamic_update_index_in_dim(returned, current + rounded, expert, 0)

    returned = lax.fori_loop(0, DEVICES, slice_term, jnp.zeros((EXPERTS, slot_total, D), jnp.float32))
    picked = returned[pair_ids, slot_row]
    weighted = picked * route_weights.reshape(N_CTX, 2 * CT)[..., None]
    grad_moe_in = jnp.sum(weighted.reshape(SEQ, 2, D), axis=1).astype(jnp.bfloat16)
    return grad_queries, grad_keys, grad_values, grad_moe_in
```

```python
import jax
import jax.numpy as jnp
from jax import lax
from jax.experimental import pallas as pl
from jax.experimental.pallas import tpu as pltpu
from jax.sharding import PartitionSpec as P

EXPERTS = 8
HEAD = 128
CAP = 36
PAD = 48
CT = 128
N_CTX = 32
HEADS = 3
WINDOW = 10
CHIPS = 16
SUBS = 3
SUB = 96
BLOCK = 288
COLS = 384
HALF = 1536
WIDE = 3072
HID = 512
MESH = pl.DeviceIdType.MESH
F32 = jnp.float32
BF16 = jnp.bfloat16
NT = (((1,), (1,)), ((), ()))
NN = (((1,), (0,)), ((), ()))
TN = (((0,), (0,)), ((), ()))


def dot(a, b, dims):
    return lax.dot_general(a, b, dims, preferred_element_type=F32)


def kernel(
    q_ref, k_ref, v_ref, ao_ref, go_ref, seg_ref, gm_ref, ids_ref, rw_ref,
    sg_ref, su_ref, wg_ref, wu_ref, wd_ref,
    dq_ref, dk_ref, dv_ref, dm_ref,
    kv, st, q3, g3, dkv, dks, dacc,
    gm, packed, arrive, arr, sg, su, wg, wu, wd,
    part, sib, b1, b2, b3s, b3, fin, unpacked, ret,
    ld_sem, kv_s, kv_r, kf_s, kf_r, ds_s, ds_r, da_s, da_r,
    pa_s, pa_r, g1_s, g1_r, g2_s, g2_r, g3_s, g3_r, g4_s, g4_r,
    r0_s, r0_r, r1_s, r1_r, r2_s, r2_r, r3_s, r3_r, pr_s, pr_r,
):
    c = lax.axis_index("ctx")
    u = lax.axis_index("tp")
    core = c % 2
    chip = c // 2
    zp = chip % 2
    xh = u // 4
    y = u % 4
    quarter = c % 4
    sibling = (c + 1 - 2 * core, u)
    first = (c + core * (2 - 4 * zp), u + (1 - core) * (4 - 8 * xh))
    last = (c + (1 - core) * (2 - 4 * zp), u + core * (4 - 8 * xh))

    def along_y(dy):
        return (c, xh * 4 + (y + dy) % 4)

    def send(src, dst, ss, rs, to):
        pltpu.make_async_remote_copy(
            src_ref=src, dst_ref=dst, send_sem=ss, recv_sem=rs,
            device_id=to, device_id_type=MESH,
        ).start()

    def got(dst, ss, rs):
        pltpu.make_async_remote_copy(
            src_ref=dst, dst_ref=dst, send_sem=ss, recv_sem=rs,
            device_id=sibling, device_id_type=MESH,
        ).wait_recv()

    def sent(src, ss, rs):
        pltpu.make_async_remote_copy(
            src_ref=src, dst_ref=src, send_sem=ss, recv_sem=rs,
            device_id=sibling, device_id_type=MESH,
        ).wait_send()

    barrier = pltpu.get_barrier_semaphore()

    @pl.loop(0, N_CTX)
    def _(i):
        @pl.when(i != c)
        def _():
            pl.semaphore_signal(barrier, inc=1, device_id=(i, u), device_id_type=MESH)

    for dy in (1, 2, 3):
        pl.semaphore_signal(barrier, inc=1, device_id=along_y(dy), device_id_type=MESH)
    pl.semaphore_signal(
        barrier, inc=1, device_id=(c, u + 4 - 8 * xh), device_id_type=MESH
    )

    own_cols = pl.ds(pl.multiple_of(u * COLS, 128), COLS)
    loads = [
        (gm_ref.at[:, own_cols], gm),
        (wd_ref, wd),
        (sg_ref, sg),
        (su_ref, su),
        (wg_ref, wg),
        (wu_ref, wu),
    ]

    def load(i):
        return pltpu.make_async_copy(loads[i][0], loads[i][1], ld_sem.at[i])

    for i in range(len(loads)):
        load(i).start()

    lane = lax.broadcasted_iota(jnp.int32, (CT, CT), 1)
    sub = lax.broadcasted_iota(jnp.int32, (CT, CT), 0)
    ids = ids_ref[...]
    hot = [(ids[:, k : k + 1] == lane).astype(F32) for k in range(2)]
    before = (lane < sub).astype(BF16)
    count = dot(before, (hot[0] + hot[1]).astype(BF16), NN)
    place = count + (PAD * lane).astype(F32)
    slot_lane = lax.broadcasted_iota(jnp.int32, (CT, EXPERTS * PAD), 1)
    pick = []
    for k in range(2):
        slot = jnp.sum(hot[k] * place, axis=1, keepdims=True).astype(jnp.int32)
        pick.append((slot_lane == slot).astype(F32))
    selector = jnp.transpose(pick[0] + pick[1]).astype(BF16)
    load(0).wait()
    packed[...] = dot(selector, gm[...], NN).astype(BF16).reshape(EXPERTS, PAD, COLS)
    kv[0, core, :, :HEAD] = k_ref[...]
    kv[0, core, :, HEAD:] = v_ref[...]

    pl.semaphore_wait(barrier, N_CTX - 1 + 4)

    source_part = c // 8
    source_slot = c % 8
    expert = c // 4

    @pl.loop(0, EXPERTS)
    def _(e):
        to = 4 * e + source_part

        @pl.when(to == c)
        def _():
            pltpu.make_async_copy(
                packed.at[e], arrive.at[source_slot], pa_r.at[source_slot]
            ).start()

        @pl.when(to != c)
        def _():
            send(packed.at[e], arrive.at[source_slot], pa_s.at[e], pa_r.at[source_slot], (to, u))

    later = jnp.minimum(WINDOW, CHIPS - 1 - chip) + 1
    earlier = jnp.minimum(WINDOW, chip) + 1

    send(kv.at[0, core], kv.at[0, core], kf_s.at[0], kf_r.at[0], sibling)

    @pl.loop(1, later)
    def _(d):
        send(kv.at[0, core], kv.at[d, core], kv_s.at[d], kv_r.at[d], (c + 2 * d, u))

    q3[...] = jnp.concatenate([q_ref[:, h * HEAD : (h + 1) * HEAD] for h in range(HEADS)], axis=0)
    g3[...] = jnp.concatenate([go_ref[:, h * HEAD : (h + 1) * HEAD] for h in range(HEADS)], axis=0)
    a3 = jnp.concatenate([ao_ref[:, h * HEAD : (h + 1) * HEAD] for h in range(HEADS)], axis=0)
    row_dots = jnp.sum(
        jnp.transpose(g3[...].astype(F32) * a3.astype(F32)), axis=0, keepdims=True
    )
    segs = seg_ref[...]
    starts = [
        jnp.sum((segs < k).astype(F32)).astype(jnp.int32) for k in (1, 2)
    ]
    own_seg = seg_ref[pl.ds(c, 1), :]
    start = jnp.where(own_seg == 0, 0, jnp.where(own_seg == 1, starts[0], starts[1]))
    start = jnp.concatenate([start] * HEADS, axis=1)
    own_pos = c * CT + lax.broadcasted_iota(jnp.int32, (1, CT), 1)
    own_pos = jnp.concatenate([own_pos] * HEADS, axis=1)

    @pl.loop(0, 8)
    def _(i):
        got(arrive.at[i], pa_s.at[i], pa_r.at[i])

    def dense_map(shape, row_axis):
        rows = lax.broadcasted_iota(jnp.int32, shape, row_axis)
        slots = lax.broadcasted_iota(jnp.int32, shape, 1 - row_axis)
        block = sum((rows >= CAP * i).astype(jnp.int32) for i in range(1, 8))
        return (slots == rows + (PAD - CAP) * block).astype(BF16)

    arr[quarter, :, own_cols] = dot(
        dense_map((BLOCK, 8 * PAD), 0), arrive[...].reshape(8 * PAD, COLS), NN
    ).astype(BF16)

    def at_block(k, fr, lr):
        dz = lr * (1 - k) + fr * k
        dx = fr * (1 - k) + lr * k
        return 2 * (zp + dz * (1 - 2 * zp)) + k, xh + dx * (1 - 2 * xh)

    def block(ref, s, k, fr, lr):
        row, col = at_block(k, fr, lr)
        return ref.at[row, pl.ds(s * SUB, SUB), pl.ds(pl.multiple_of(col * HALF, 128), HALF)]

    def piece(ref, s, fr, py):
        row, col = at_block(core, fr, 0)
        return ref.at[
            row, pl.ds(s * SUB, SUB), pl.ds(pl.multiple_of(col * HALF + py * COLS, 128), COLS)
        ]

    def gather_1(s):
        own = piece(arr, s, 0, y)
        send(own, own, g1_s.at[s], g1_r.at[s], first)
        for dy in (1, 2, 3):
            send(own, own, g2_s.at[s, 0, dy], g2_r.at[s, 0, dy], along_y(dy))

    def gather_2(s):
        other = piece(arr, s, 1, y)
        got(other, g1_s.at[s], g1_r.at[s])
        for dy in (1, 2, 3):
            send(other, other, g2_s.at[s, 1, dy], g2_r.at[s, 1, dy], along_y(dy))

    def gather_3(s):
        for fr in (0, 1):
            for dy in (1, 2, 3):
                got(piece(arr, s, fr, (y + 4 - dy) % 4), g2_s.at[s, fr, dy], g2_r.at[s, fr, dy])
            whole = block(arr, s, core, fr, 0)
            send(whole, whole, g3_s.at[s, fr], g3_r.at[s, fr], last)
            send(whole, whole, g4_s.at[s, fr, 0], g4_r.at[s, fr, 0], sibling)

    def gather_4(s):
        for fr in (0, 1):
            whole = block(arr, s, core, fr, 1)
            got(whole, g3_s.at[s, fr], g3_r.at[s, fr])
            send(whole, whole, g4_s.at[s, fr, 1], g4_r.at[s, fr, 1], sibling)

    def gather_5(s):
        for fr in (0, 1):
            for lr in (0, 1):
                got(block(arr, s, 1 - core, fr, lr), g4_s.at[s, fr, lr], g4_r.at[s, fr, lr])

    def expert_rows(s):
        rows = pl.ds(s * SUB, SUB)
        hidden = dot(arr[:, rows, :].reshape(4 * SUB, WIDE), wd[...], NT)
        gate = sg[:, rows, :].reshape(4 * SUB, HID).astype(F32)
        up = su[:, rows, :].reshape(4 * SUB, HID).astype(F32)
        sig = jax.nn.sigmoid(gate)
        hs = hidden * sig
        grad_up = (hs * gate).astype(BF16)
        grad_gate = (hs * up * (1.0 + gate * (1.0 - sig))).astype(BF16)

        @pl.loop(0, WIDE // HID)
        def _(n):
            cols = pl.ds(pl.multiple_of(n * HID, HID), HID)
            out = dot(grad_gate, wg[cols, :], NT) + dot(grad_up, wu[cols, :], NT)
            part[:, rows, cols] = out.astype(BF16).reshape(4, SUB, HID)

    def return_0(s):
        for i in (0, 1):
            send(
                part.at[2 * i + 1 - core, pl.ds(s * SUB, SUB)],
                sib.at[i, pl.ds(s * SUB, SUB)],
                r0_s.at[s, i], r0_r.at[s, i], sibling,
            )

    def sib_block(s, fr, lr):
        row, col = at_block(core, fr, lr)
        return sib[
            row // 2, pl.ds(s * SUB, SUB), pl.ds(pl.multiple_of(col * HALF, 128), HALF)
        ].astype(F32)

    def return_1(s):
        for i in (0, 1):
            got(sib.at[i, pl.ds(s * SUB, SUB)], r0_s.at[s, i], r0_r.at[s, i])
        for fr in (1, 0):
            mine = block(part, s, core, fr, 1)
            mine[...] = (mine[...].astype(F32) + sib_block(s, fr, 1)).astype(BF16)
            send(mine, b1.at[s, fr], r1_s.at[s, fr], r1_r.at[s, fr], last)

    def return_2(s):
        for fr in (1, 0):
            got(b1.at[s, fr], r1_s.at[s, fr], r1_r.at[s, fr])
            mine = block(part, s, core, fr, 0)
            mine[...] = (
                mine[...].astype(F32) + sib_block(s, fr, 0) + b1[s, fr].astype(F32)
            ).astype(BF16)
            for dy in (1, 2, 3):
                send(
                    piece(part, s, fr, (y + dy) % 4), b2.at[s, fr, dy - 1],
                    r2_s.at[s, fr, dy], r2_r.at[s, fr, dy], along_y(dy),
                )

    def y_sum(s, fr):
        for dy in (1, 2, 3):
            got(b2.at[s, fr, dy - 1], r2_s.at[s, fr, dy], r2_r.at[s, fr, dy])
        total = piece(part, s, fr, y)[...].astype(F32)
        for i in range(3):
            total = total + b2[s, fr, i].astype(F32)
        return total

    def return_3(s):
        b3s[s] = y_sum(s, 1).astype(BF16)
        send(b3s.at[s], b3.at[s], r3_s.at[s], r3_r.at[s], first)

    def return_4(s):
        total = y_sum(s, 0)
        got(b3.at[s], r3_s.at[s], r3_r.at[s])
        fin[pl.ds(s * SUB, SUB), :] = (total + b3[s].astype(F32)).astype(BF16)

    def keys_forward():
        @pl.loop(1, earlier)
        def _(d):
            mine = kv.at[d, core]
            got(mine, kv_s.at[d], kv_r.at[d])
            send(mine, mine, kf_s.at[d], kf_r.at[d], sibling)

    def keys_of(d):
        return kv[d, :, :, :HEAD].reshape(2 * CT, HEAD)

    def scores_pass():
        def step(d, top):
            got(kv.at[d, 1 - core], kf_s.at[d], kf_r.at[d])
            s = dot(keys_of(d), q3[...], NT) * (HEAD ** -0.5)
            pos = (chip - d) * 2 * CT + lax.broadcasted_iota(jnp.int32, (2 * CT, 1), 0)
            s = jnp.where((pos <= own_pos) & (pos >= start), s, -1e30)
            st[d] = s
            return jnp.maximum(top, jnp.max(s, axis=0, keepdims=True))

        top = lax.fori_loop(0, earlier, step, jnp.full((1, HEADS * CT), -1e30, F32))

        def step_2(d, total):
            p = jnp.exp(st[d] - top)
            st[d] = p
            return total + jnp.sum(p, axis=0, keepdims=True)

        total = lax.fori_loop(0, earlier, step_2, jnp.zeros((1, HEADS * CT), F32))
        return 1.0 / total

    def grads_pass(inverse):
        def step(d, dqt):
            probs = st[d] * inverse
            keys = keys_of(d)
            values = kv[d, :, :, HEAD:].reshape(2 * CT, HEAD)
            grad_probs = dot(values, g3[...], NT)
            grad_scores = (probs * (grad_probs - row_dots)).astype(BF16)
            dkv[d, :, :, :HEAD] = (
                (dot(grad_scores, q3[...], NN) * (HEAD ** -0.5)).astype(BF16).reshape(2, CT, HEAD)
            )
            dkv[d, :, :, HEAD:] = (
                dot(probs.astype(BF16), g3[...], NN).astype(BF16).reshape(2, CT, HEAD)
            )
            send(dkv.at[d, 1 - core], dks.at[d], ds_s.at[d], ds_r.at[d], sibling)
            return dqt + dot(keys, grad_scores, TN)

        dqt = lax.fori_loop(0, earlier, step, jnp.zeros((HEAD, HEADS * CT), F32))
        dq = jnp.transpose(dqt * (HEAD ** -0.5)).astype(BF16)
        for h in range(HEADS):
            dq_ref[:, h * HEAD : (h + 1) * HEAD] = dq[h * CT : (h + 1) * CT, :]

    def keys_return():
        @pl.loop(0, earlier)
        def _(d):
            got(dks.at[d], ds_s.at[d], ds_r.at[d])
            dkv[d, core] = (dkv[d, core].astype(F32) + dks[d].astype(F32)).astype(BF16)

            @pl.when(d > 0)
            def _():
                send(dkv.at[d, core], dacc.at[d], da_s.at[d], da_r.at[d], (c - 2 * d, u))

    def keys_finish():
        def step(d, total):
            got(dacc.at[d], da_s.at[d], da_r.at[d])
            return total + dacc[d].astype(F32)

        total = lax.fori_loop(1, later, step, dkv[0, core].astype(F32))
        dk_ref[...] = total[:, :HEAD].astype(BF16)
        dv_ref[...] = total[:, HEAD:].astype(BF16)

    for s in range(SUBS):
        gather_1(s)
    keys_forward()
    for s in range(SUBS):
        gather_2(s)
    inverse = scores_pass()
    gather_3(0)
    grads_pass(inverse)
    gather_3(1)
    gather_4(0)
    for i in range(1, 6):
        load(i).wait()
    gather_5(0)
    expert_rows(0)
    return_0(0)
    gather_3(2)
    gather_4(1)
    keys_return()
    gather_5(1)
    expert_rows(1)
    return_0(1)
    gather_4(2)
    return_1(0)
    gather_5(2)
    expert_rows(2)
    return_0(2)
    return_1(1)
    return_2(0)
    return_1(2)
    return_2(1)
    return_3(0)
    return_2(2)
    return_4(0)
    return_3(1)
    return_4(1)
    return_3(2)
    keys_finish()
    return_4(2)

    unpacked[...] = (
        dot(dense_map((8 * PAD, BLOCK), 1), fin[...], NN).astype(BF16).reshape(8, PAD, COLS)
    )

    @pl.loop(0, 8)
    def _(i):
        to = 8 * quarter + i

        @pl.when(to == c)
        def _():
            pltpu.make_async_copy(unpacked.at[i], ret.at[expert], pr_r.at[expert]).start()

        @pl.when(to != c)
        def _():
            send(unpacked.at[i], ret.at[expert], pr_s.at[i], pr_r.at[expert], (to, u))

    for s in range(SUBS):
        sent(piece(arr, s, 0, y), g1_s.at[s], g1_r.at[s])
        sent(b3s.at[s], r3_s.at[s], r3_r.at[s])
        for fr in (0, 1):
            for dy in (1, 2, 3):
                sent(piece(arr, s, fr, y), g2_s.at[s, fr, dy], g2_r.at[s, fr, dy])
                sent(b2.at[s, fr, dy - 1], r2_s.at[s, fr, dy], r2_r.at[s, fr, dy])
            sent(b1.at[s, fr], g3_s.at[s, fr], g3_r.at[s, fr])
            sent(b1.at[s, fr], r1_s.at[s, fr], r1_r.at[s, fr])
            sent(sib.at[fr, pl.ds(s * SUB, SUB)], r0_s.at[s, fr], r0_r.at[s, fr])
            for lr in (0, 1):
                sent(b1.at[s, fr], g4_s.at[s, fr, lr], g4_r.at[s, fr, lr])
    sent(kv.at[0, core], kf_s.at[0], kf_r.at[0])
    sent(dkv.at[0, core], ds_s.at[0], ds_r.at[0])

    @pl.loop(1, later)
    def _(d):
        sent(kv.at[0, core], kv_s.at[d], kv_r.at[d])

    @pl.loop(1, earlier)
    def _(d):
        sent(kv.at[d, core], kf_s.at[d], kf_r.at[d])
        sent(dkv.at[d, 1 - core], ds_s.at[d], ds_r.at[d])
        sent(dkv.at[d, core], da_s.at[d], da_r.at[d])

    @pl.loop(0, 8)
    def _(i):
        @pl.when(4 * i + source_part != c)
        def _():
            sent(packed.at[i], pa_s.at[i], pa_r.at[i])

        @pl.when(8 * quarter + i != c)
        def _():
            sent(unpacked.at[i], pr_s.at[i], pr_r.at[i])

    @pl.loop(0, EXPERTS)
    def _(i):
        got(ret.at[i], pr_s.at[i], pr_r.at[i])

    rows = ret[...].reshape(EXPERTS * PAD, COLS)
    weights = rw_ref[...]
    dm_ref[...] = sum(
        weights[:, k : k + 1] * dot(pick[k].astype(BF16), rows, NN) for k in range(2)
    ).astype(BF16)


def per_device(
    queries, key_rows, value_rows, attn_out, grad_out, segments, grad_moe_out,
    expert_ids, route_weights, saved_gate, saved_up, w_gate, w_up, w_down,
):
    vmem = pl.BlockSpec(memory_space=pltpu.VMEM)
    hbm = pl.BlockSpec(memory_space=pl.ANY)
    dma = pltpu.SemaphoreType.DMA
    slots = WINDOW + 1
    shapes = [
        jax.ShapeDtypeStruct((CT, HEADS * HEAD), BF16),
        jax.ShapeDtypeStruct((CT, HEAD), BF16),
        jax.ShapeDtypeStruct((CT, HEAD), BF16),
        jax.ShapeDtypeStruct((CT, COLS), BF16),
    ]
    scratch = [
        pltpu.VMEM((slots, 2, CT, 2 * HEAD), BF16),
        pltpu.VMEM((slots, 2 * CT, HEADS * CT), F32),
        pltpu.VMEM((HEADS * CT, HEAD), BF16),
        pltpu.VMEM((HEADS * CT, HEAD), BF16),
        pltpu.VMEM((slots, 2, CT, 2 * HEAD), BF16),
        pltpu.VMEM((slots, CT, 2 * HEAD), BF16),
        pltpu.VMEM((slots, CT, 2 * HEAD), BF16),
        pltpu.VMEM((CT, COLS), BF16),
        pltpu.VMEM((EXPERTS, PAD, COLS), BF16),
        pltpu.VMEM((8, PAD, COLS), BF16),
        pltpu.VMEM((4, BLOCK, WIDE), BF16),
        pltpu.VMEM((4, BLOCK, HID), BF16),
        pltpu.VMEM((4, BLOCK, HID), BF16),
        pltpu.VMEM((WIDE, HID), BF16),
        pltpu.VMEM((WIDE, HID), BF16),
        pltpu.VMEM((HID, WIDE), BF16),
        pltpu.VMEM((4, BLOCK, WIDE), BF16),
        pltpu.VMEM((2, BLOCK, WIDE), BF16),
        pltpu.VMEM((SUBS, 2, SUB, HALF), BF16),
        pltpu.VMEM((SUBS, 2, 3, SUB, COLS), BF16),
        pltpu.VMEM((SUBS, SUB, COLS), BF16),
        pltpu.VMEM((SUBS, SUB, COLS), BF16),
        pltpu.VMEM((BLOCK, COLS), BF16),
        pltpu.VMEM((8, PAD, COLS), BF16),
        pltpu.VMEM((EXPERTS, PAD, COLS), BF16),
        dma((6,)),
    ]
    for shape in (
        (slots,), (slots,), (slots,), (slots,),
        (8,),
        (SUBS,), (SUBS, 2, 4), (SUBS, 2), (SUBS, 2, 2),
        (SUBS, 2), (SUBS, 2), (SUBS, 2, 4), (SUBS,),
        (8,),
    ):
        scratch += [dma(shape), dma(shape)]
    return pl.pallas_call(
        kernel,
        out_shape=shapes,
        in_specs=[vmem] * 6 + [hbm] + [vmem] * 2 + [hbm] * 5,
        out_specs=[vmem] * 4,
        scratch_shapes=scratch,
        compiler_params=pltpu.CompilerParams(
            collective_id=0, has_side_effects=True, vmem_limit_bytes=60 * 2**20
        ),
        cost_estimate=pl.CostEstimate(
            flops=13 * 10**9, bytes_accessed=12 * 10**6, transcendentals=2 * 10**6
        ),
    )(
        queries, key_rows, value_rows, attn_out, grad_out,
        segments.reshape(N_CTX, CT), grad_moe_out, expert_ids, route_weights,
        saved_gate.reshape(4, BLOCK, HID), saved_up.reshape(4, BLOCK, HID),
        w_gate, w_up, w_down,
    )


def solution(mesh):
    in_specs = (
        P("ctx", "tp"), P("ctx", "tp"), P("ctx", "tp"), P("ctx", "tp"), P("ctx", "tp"),
        P(), P("ctx", None), P("ctx", None), P("ctx", None),
        P("ctx", "tp"), P("ctx", "tp"),
        P(None, ("ctx", "tp")), P(None, ("ctx", "tp")), P(("ctx", "tp"), None),
    )
    out_specs = (P("ctx", "tp"), P("ctx", "tp"), P("ctx", "tp"), P("ctx", "tp"))
    return jax.shard_map(
        per_device, mesh=mesh, in_specs=in_specs, out_specs=out_specs, check_vma=False
    )
```

```python
import jax
import jax.numpy as jnp
import numpy as np
from jax import lax
from jax.experimental import pallas as pl
from jax.experimental.pallas import tpu as pltpu
from jax.sharding import PartitionSpec as P

EXPERTS = 8
HEAD = 128
CAP = 36
THIRD = 12
TILE = 16
SPREAD = 8 * TILE
CT = 128
N_CTX = 32
HEADS = 3
WINDOW = 10
CHIPS = 16
SUBS = 3
SUB = 96
Y_LAST = ()
BLOCK = 288
SET = 144
COLS = 384
HALF = 1536
WIDE = 3072
HID = 512
MESH = pl.DeviceIdType.MESH
F32 = jnp.float32
BF16 = jnp.bfloat16
NT = (((1,), (1,)), ((), ()))
NN = (((1,), (0,)), ((), ()))
TN = (((0,), (0,)), ((), ()))


def dot(a, b, dims):
    return lax.dot_general(a, b, dims, preferred_element_type=F32)


def kernel(
    q_ref, k_ref, v_ref, ao_ref, go_ref, seg_ref, gm_ref, ids_ref, rw_ref,
    sg_ref, su_ref, perm_ref, wg_ref, wu_ref, wd_ref,
    dq_ref, dk_ref, dv_ref, dm_ref,
    kv, st, q3, g3, dkv, dks, dacc,
    gm, packed, arrive, arr, sgr, sur, perm, sg, su, sgx, sux, wg, wu, wd,
    part, b1, b2, b3s, b3, unpacked, ret,
    ld_sem, kv_s, kv_r, kf_s, kf_r, ds_s, ds_r, da_s, da_r,
    pa_s, pa_r, g1_s, g1_r, g2_s, g2_r, g3_s, g3_r, w_s, w_r,
    x_s, x_r, r1_s, r1_r, r2_s, r2_r, r3_s, r3_r, pr_s, pr_r,
):
    c = lax.axis_index("ctx")
    u = lax.axis_index("tp")
    core = c % 2
    chip = c // 2
    zp = chip % 2
    xh = u // 4
    y = u % 4
    quarter = c % 4
    sibling = (c + 1 - 2 * core, u)
    first = (c + core * (2 - 4 * zp), u + (1 - core) * (4 - 8 * xh))
    last = (c + (1 - core) * (2 - 4 * zp), u + core * (4 - 8 * xh))

    def along_y(dy):
        return (c, xh * 4 + (y + dy) % 4)

    def send(src, dst, ss, rs, to):
        pltpu.make_async_remote_copy(
            src_ref=src, dst_ref=dst, send_sem=ss, recv_sem=rs,
            device_id=to, device_id_type=MESH,
        ).start()

    def got(dst, ss, rs):
        pltpu.make_async_remote_copy(
            src_ref=dst, dst_ref=dst, send_sem=ss, recv_sem=rs,
            device_id=sibling, device_id_type=MESH,
        ).wait_recv()

    def sent(src, ss, rs):
        pltpu.make_async_remote_copy(
            src_ref=src, dst_ref=src, send_sem=ss, recv_sem=rs,
            device_id=sibling, device_id_type=MESH,
        ).wait_send()

    barrier = pltpu.get_barrier_semaphore()

    for i in range(1, N_CTX):
        pl.semaphore_signal(
            barrier, inc=1, device_id=((c + i) % N_CTX, u), device_id_type=MESH
        )
    for dy in (1, 2, 3):
        pl.semaphore_signal(barrier, inc=1, device_id=along_y(dy), device_id_type=MESH)
    pl.semaphore_signal(
        barrier, inc=1, device_id=(c, u + 4 - 8 * xh), device_id_type=MESH
    )

    own_cols = pl.ds(pl.multiple_of(u * COLS, 128), COLS)
    expert = c // 4
    rank_pair = expert % 4
    loads = [(gm_ref.at[:, own_cols], gm), (perm_ref, perm)]
    for x in (0, 1):
        for diff in range(4):
            group = 4 * x + (rank_pair + 4 - diff) % 4
            loads += [(sg_ref.at[group], sgr.at[x, diff]), (su_ref.at[group], sur.at[x, diff])]
    weights = [(wd_ref, wd.at[core]), (wg_ref, wg.at[core]), (wu_ref, wu.at[core])]
    loads += weights

    def load(i):
        return pltpu.make_async_copy(loads[i][0], loads[i][1], ld_sem.at[i])

    for i in range(len(loads)):
        load(i).start()

    ids = ids_ref[...]
    expert_row = lax.broadcasted_iota(jnp.int32, (EXPERTS, CT), 0)
    hot = [(ids[k : k + 1, :] == expert_row).astype(F32) for k in range(2)]
    before = (
        lax.broadcasted_iota(jnp.int32, (CT, CT), 0) < lax.broadcasted_iota(jnp.int32, (CT, CT), 1)
    ).astype(BF16)
    rank = dot((hot[0] + hot[1]).astype(BF16), before, NN)
    third = (rank >= THIRD).astype(F32) + (rank >= 2 * THIRD).astype(F32)
    place = rank + (SPREAD - THIRD) * third + (TILE * expert_row).astype(F32)
    slot_row = lax.broadcasted_iota(jnp.int32, (SUBS * SPREAD, CT), 0)
    pick = []
    for k in range(2):
        slot = jnp.sum(hot[k] * place, axis=0, keepdims=True).astype(jnp.int32)
        pick.append((slot_row == slot).astype(F32))
    selector = (pick[0] + pick[1]).astype(BF16)
    load(0).wait()
    packed[...] = dot(selector, gm[...], NN).astype(BF16).reshape(SUBS, EXPERTS, TILE, COLS)
    kv[0, core, :, :HEAD] = k_ref[...]
    kv[0, core, :, HEAD:] = v_ref[...]

    pl.semaphore_wait(barrier, N_CTX - 1 + 4)

    own_x = c // 16
    own_pair = (chip % 8) // 2
    for s in range(SUBS):

        @pl.loop(0, EXPERTS)
        def _(e):
            diff = (e % 4 - own_pair + 4) % 4
            to_z = (1 - zp) * (diff // 2) + zp * (((diff + 1) // 2 + 1) % 2)
            slot = 4 * own_x + (1 - zp) * (diff % 2) + zp * (2 + diff // 2)
            to = ((e // 4) * 8 + 2 * (e % 4) + to_z) * 2 + core

            @pl.when(e == expert)
            def _():
                pltpu.make_async_copy(
                    packed.at[s, e], arrive.at[s, slot], pa_r.at[s, slot]
                ).start()

            @pl.when(e != expert)
            def _():
                send(
                    packed.at[s, e], arrive.at[s, slot],
                    pa_s.at[s, e], pa_r.at[s, slot], (to, u),
                )

    later = jnp.minimum(WINDOW, CHIPS - 1 - chip) + 1
    earlier = jnp.minimum(WINDOW, chip) + 1

    send(kv.at[0, core], kv.at[0, core], kf_s.at[0], kf_r.at[0], sibling)

    @pl.loop(1, later)
    def _(d):
        send(kv.at[0, core], kv.at[d, core], kv_s.at[d], kv_r.at[d], (c + 2 * d, u))

    for i, (src, dst) in enumerate(weights):
        send(src, dst, w_s.at[i], w_r.at[i], sibling)

    q3[...] = jnp.concatenate([q_ref[:, h * HEAD : (h + 1) * HEAD] for h in range(HEADS)], axis=0)
    g3[...] = jnp.concatenate([go_ref[:, h * HEAD : (h + 1) * HEAD] for h in range(HEADS)], axis=0)
    a3 = jnp.concatenate([ao_ref[:, h * HEAD : (h + 1) * HEAD] for h in range(HEADS)], axis=0)
    row_dots = jnp.sum(
        jnp.transpose(g3[...].astype(F32) * a3.astype(F32)), axis=0, keepdims=True
    )
    segs = seg_ref[...]
    starts = [
        jnp.sum((segs < k).astype(F32)).astype(jnp.int32) for k in (1, 2)
    ]
    own_seg = seg_ref[pl.ds(c, 1), :]
    start = jnp.where(own_seg == 0, 0, jnp.where(own_seg == 1, starts[0], starts[1]))
    start = jnp.concatenate([start] * HEADS, axis=1)
    own_pos = c * CT + lax.broadcasted_iota(jnp.int32, (1, CT), 1)
    own_pos = jnp.concatenate([own_pos] * HEADS, axis=1)

    def order_saved():
        for i in range(1, 18):
            load(i).wait()
        for raw, ordered in ((sgr, sg), (sur, su)):
            for x in (0, 1):
                rows = dot(perm[...], raw[x].reshape(4 * SET, HID), NN).astype(BF16)
                ordered[:, :, :, x] = rows.reshape(2, 2, SUBS, SUB // 2, HID)
        for i, (src, dst) in enumerate(((sg, sgx), (su, sux))):
            for j in (0, 1):
                send(src.at[j, 1 - core], dst.at[j], x_s.at[i, j], x_r.at[i, j], sibling)

    def dense_map(shape, row_axis):
        rows = lax.broadcasted_iota(jnp.int32, shape, row_axis)
        slots = lax.broadcasted_iota(jnp.int32, shape, 1 - row_axis)
        group = sum((rows >= THIRD * i).astype(jnp.int32) for i in range(1, 8))
        return (slots == rows + (TILE - THIRD) * group).astype(BF16)

    def dense(s):
        @pl.loop(0, 8)
        def _(i):
            got(arrive.at[s, i], pa_s.at[s, i], pa_r.at[s, i])

        arr[zp, s * SUB : (s + 1) * SUB, own_cols] = dot(
            dense_map((SUB, SPREAD), 0), arrive[s].reshape(SPREAD, COLS), NN
        ).astype(BF16)

    def at_block(fr, lr):
        dz = lr * (1 - core) + fr * core
        dx = fr * (1 - core) + lr * core
        return zp + dz * (1 - 2 * zp), xh + dx * (1 - 2 * xh)

    def piece(ref, s, fr, lr, py):
        row, col = at_block(fr, lr)
        return ref.at[
            row, pl.ds(s * SUB, SUB), pl.ds(pl.multiple_of(col * HALF + py * COLS, 128), COLS)
        ]

    def y_at(dy):
        return (y + dy) % 4

    def to_last(s, fr, dy):
        mine = piece(arr, s, fr, 0, y_at(4 - dy))
        send(mine, mine, g3_s.at[s, fr, dy], g3_r.at[s, fr, dy], last)

    def to_y(s, fr, lr):
        mine = piece(arr, s, fr, lr, y)
        for dy in (1, 2, 3):
            send(mine, mine, g2_s.at[s, fr, lr, dy], g2_r.at[s, fr, lr, dy], along_y(dy))

    def from_y(s, fr, lr, dy):
        got(
            piece(arr, s, fr, lr, y_at(4 - dy)),
            g2_s.at[s, fr, lr, dy], g2_r.at[s, fr, lr, dy],
        )

    def from_last(s, fr, dy):
        got(piece(arr, s, fr, 1, y_at(4 - dy)), g3_s.at[s, fr, dy], g3_r.at[s, fr, dy])

    def gather_1(s):
        dense(s)
        mine = piece(arr, s, 0, 0, y)
        send(mine, mine, g1_s.at[s], g1_r.at[s], first)
        to_y(s, 0, 0)
        to_last(s, 0, 0)

    def gather_2(s):
        got(piece(arr, s, 1, 0, y), g1_s.at[s], g1_r.at[s])
        to_y(s, 1, 0)
        to_last(s, 1, 0)

    def gather_3(s):
        for fr in (0, 1):
            if s in Y_LAST:
                from_last(s, fr, 0)
                to_y(s, fr, 1)
            else:
                for dy in (1, 2, 3):
                    from_y(s, fr, 0, dy)
                    to_last(s, fr, dy)

    def gather_4(s):
        for fr in (0, 1):
            for lr in (0, 1) if s in Y_LAST else (1,):
                for dy in range(4):
                    if s not in Y_LAST:
                        from_last(s, fr, dy)
                    elif dy > 0:
                        from_y(s, fr, lr, dy)

    def wait_weights():
        for i in range(18, 21):
            load(i).wait()
        for i, (src, _) in enumerate(weights):
            got((wd, wg, wu)[i].at[1 - core], w_s.at[i], w_r.at[i])
        for i, dst in enumerate((sgx, sux)):
            for j in (0, 1):
                got(dst.at[j], x_s.at[i, j], x_r.at[i, j])

    def expert_rows(s):
        rows = pl.ds(s * SUB, SUB)
        grads = []
        for k, gate, up in (
            (core, sg[:, core, s], su[:, core, s]),
            (1 - core, sgx[:, s], sux[:, s]),
        ):
            hidden = dot(arr[:, rows, :].reshape(2 * SUB, WIDE), wd[k], NT)
            gate = gate.reshape(2 * SUB, HID).astype(F32)
            up = up.reshape(2 * SUB, HID).astype(F32)
            sig = jax.nn.sigmoid(gate)
            hs = hidden * sig
            grad_up = (hs * gate).astype(BF16)
            grad_gate = (hs * up * (1.0 + gate * (1.0 - sig))).astype(BF16)
            grads.append((k, grad_gate, grad_up))

        @pl.loop(0, WIDE // HID)
        def _(n):
            cols = pl.ds(pl.multiple_of(n * HID, HID), HID)
            out = sum(
                dot(grad_gate, wg[k, cols, :], NT) + dot(grad_up, wu[k, cols, :], NT)
                for k, grad_gate, grad_up in grads
            )
            part[:, rows, cols] = out.astype(BF16).reshape(2, SUB, HID)

    def part_at(s, fr, lr, py):
        row, col = at_block(fr, lr)
        cols = pl.ds(pl.multiple_of(col * HALF + py * COLS, 128), COLS)
        return part[row, pl.ds(s * SUB, SUB), cols].astype(F32)

    def half_to_last(s, fr, dy):
        mine = piece(part, s, fr, 1, y_at(dy))
        send(mine, b1.at[s, fr, dy], r1_s.at[s, fr, dy], r1_r.at[s, fr, dy], last)

    def half_to_y(s, fr, lr, dy):
        send(
            piece(part, s, fr, lr, y_at(dy)), b2.at[s, fr, lr, dy - 1],
            r2_s.at[s, fr, lr, dy], r2_r.at[s, fr, lr, dy], along_y(dy),
        )

    def add_last(s, fr, dy):
        got(b1.at[s, fr, dy], r1_s.at[s, fr, dy], r1_r.at[s, fr, dy])
        return b1[s, fr, dy].astype(F32)

    def add_y(s, fr, lr):
        total = part_at(s, fr, lr, y)
        for dy in (1, 2, 3):
            got(b2.at[s, fr, lr, dy - 1], r2_s.at[s, fr, lr, dy], r2_r.at[s, fr, lr, dy])
            total = total + b2[s, fr, lr, dy - 1].astype(F32)
        return total

    def return_1(s):
        if s in Y_LAST:
            for lr in (1, 0):
                for fr in (1, 0):
                    for dy in (1, 2, 3):
                        half_to_y(s, fr, lr, dy)
        else:
            for dy in (1, 2, 3, 0):
                for fr in (1, 0):
                    half_to_last(s, fr, dy)

    def return_2(s):
        for fr in (1, 0):
            if s in Y_LAST:
                mine = piece(part, s, fr, 1, y)
                mine[...] = add_y(s, fr, 1).astype(BF16)
                half_to_last(s, fr, 0)
            else:
                for dy in (1, 2, 3):
                    mine = piece(part, s, fr, 0, y_at(dy))
                    total = part_at(s, fr, 0, y_at(dy)) + add_last(s, fr, dy)
                    mine[...] = total.astype(BF16)
                    half_to_y(s, fr, 0, dy)

    def return_3(s):
        b3s[s] = (add_y(s, 1, 0) + add_last(s, 1, 0)).astype(BF16)
        send(b3s.at[s], b3.at[s], r3_s.at[s], r3_r.at[s], first)

    def return_4(s):
        total = add_y(s, 0, 0) + add_last(s, 0, 0)
        got(b3.at[s], r3_s.at[s], r3_r.at[s])
        rows = (total + b3[s].astype(F32)).astype(BF16)
        unpacked[s] = (
            dot(dense_map((SPREAD, SUB), 1), rows, NN).astype(BF16).reshape(8, TILE, COLS)
        )

        @pl.loop(0, 8)
        def _(i):
            to = source_of(i)

            @pl.when(to == c)
            def _():
                pltpu.make_async_copy(
                    unpacked.at[s, i], ret.at[s, expert], pr_r.at[s, expert]
                ).start()

            @pl.when(to != c)
            def _():
                send(
                    unpacked.at[s, i], ret.at[s, expert],
                    pr_s.at[s, i], pr_r.at[s, expert], (to, u),
                )

    def source_of(i):
        at = i % 4
        from_z = at // 2
        diff = (1 - zp) * (at - from_z) + zp * ((at + 2) * (1 - from_z) + 3 * from_z * (at % 2))
        return ((i // 4) * 8 + 2 * ((rank_pair + 4 - diff) % 4) + from_z) * 2 + core

    def keys_forward():
        @pl.loop(1, earlier)
        def _(d):
            mine = kv.at[d, core]
            got(mine, kv_s.at[d], kv_r.at[d])
            send(mine, mine, kf_s.at[d], kf_r.at[d], sibling)

    def keys_of(d):
        return kv[d, :, :, :HEAD].reshape(2 * CT, HEAD)

    def scores_pass():
        def step(d, top):
            got(kv.at[d, 1 - core], kf_s.at[d], kf_r.at[d])
            s = dot(keys_of(d), q3[...], NT) * (HEAD ** -0.5)
            pos = (chip - d) * 2 * CT + lax.broadcasted_iota(jnp.int32, (2 * CT, 1), 0)
            s = jnp.where((pos <= own_pos) & (pos >= start), s, -1e30)
            st[d] = s
            return jnp.maximum(top, jnp.max(s, axis=0, keepdims=True))

        top = lax.fori_loop(0, earlier, step, jnp.full((1, HEADS * CT), -1e30, F32))

        def step_2(d, total):
            p = jnp.exp(st[d] - top)
            st[d] = p
            return total + jnp.sum(p, axis=0, keepdims=True)

        total = lax.fori_loop(0, earlier, step_2, jnp.zeros((1, HEADS * CT), F32))
        return 1.0 / total

    def grads_pass(inverse):
        def step(d, dqt):
            probs = st[d] * inverse
            keys = keys_of(d)
            values = kv[d, :, :, HEAD:].reshape(2 * CT, HEAD)
            grad_probs = dot(values, g3[...], NT)
            grad_scores = (probs * (grad_probs - row_dots)).astype(BF16)
            dkv[d, :, :, :HEAD] = (
                (dot(grad_scores, q3[...], NN) * (HEAD ** -0.5)).astype(BF16).reshape(2, CT, HEAD)
            )
            dkv[d, :, :, HEAD:] = (
                dot(probs.astype(BF16), g3[...], NN).astype(BF16).reshape(2, CT, HEAD)
            )
            send(dkv.at[d, 1 - core], dks.at[d], ds_s.at[d], ds_r.at[d], sibling)
            return dqt + dot(keys, grad_scores, TN)

        dqt = lax.fori_loop(0, earlier, step, jnp.zeros((HEAD, HEADS * CT), F32))
        dq = jnp.transpose(dqt * (HEAD ** -0.5)).astype(BF16)
        for h in range(HEADS):
            dq_ref[:, h * HEAD : (h + 1) * HEAD] = dq[h * CT : (h + 1) * CT, :]

    def keys_return():
        @pl.loop(0, earlier)
        def _(d):
            got(dks.at[d], ds_s.at[d], ds_r.at[d])
            dkv[d, core] = (dkv[d, core].astype(F32) + dks[d].astype(F32)).astype(BF16)

            @pl.when(d > 0)
            def _():
                send(dkv.at[d, core], dacc.at[d], da_s.at[d], da_r.at[d], (c - 2 * d, u))

    def keys_finish():
        def step(d, total):
            got(dacc.at[d], da_s.at[d], da_r.at[d])
            return total + dacc[d].astype(F32)

        total = lax.fori_loop(1, later, step, dkv[0, core].astype(F32))
        dk_ref[...] = total[:, :HEAD].astype(BF16)
        dv_ref[...] = total[:, HEAD:].astype(BF16)

    order_saved()
    gather_1(0)
    gather_1(1)
    gather_2(0)
    gather_1(2)
    gather_2(1)
    gather_2(2)
    gather_3(0)
    keys_forward()
    gather_3(1)
    gather_3(2)
    gather_4(0)
    wait_weights()
    expert_rows(0)
    return_1(0)
    gather_4(1)
    expert_rows(1)
    return_1(1)
    inverse = scores_pass()
    return_2(0)
    gather_4(2)
    expert_rows(2)
    return_1(2)
    grads_pass(inverse)
    return_2(1)
    return_3(0)
    return_2(2)
    keys_return()
    return_4(0)
    return_3(1)
    return_4(1)
    return_3(2)
    return_4(2)
    keys_finish()

    for s in range(SUBS):
        sent(b3s.at[s], g1_s.at[s], g1_r.at[s])
        sent(b3s.at[s], r3_s.at[s], r3_r.at[s])
        for fr in (0, 1):
            for dy in range(1 if s in Y_LAST else 4):
                sent(b3s.at[s], g3_s.at[s, fr, dy], g3_r.at[s, fr, dy])
                sent(b3s.at[s], r1_s.at[s, fr, dy], r1_r.at[s, fr, dy])
            for lr in (0, 1) if s in Y_LAST else (0,):
                for dy in (1, 2, 3):
                    sent(b3s.at[s], g2_s.at[s, fr, lr, dy], g2_r.at[s, fr, lr, dy])
                    sent(b3s.at[s], r2_s.at[s, fr, lr, dy], r2_r.at[s, fr, lr, dy])
    for i, (_, dst) in enumerate(weights):
        sent(dst, w_s.at[i], w_r.at[i])
    for i, src in enumerate((sgx, sux)):
        for j in (0, 1):
            sent(src.at[j], x_s.at[i, j], x_r.at[i, j])
    sent(kv.at[0, core], kf_s.at[0], kf_r.at[0])
    sent(dkv.at[0, core], ds_s.at[0], ds_r.at[0])

    @pl.loop(1, later)
    def _(d):
        sent(kv.at[0, core], kv_s.at[d], kv_r.at[d])

    @pl.loop(1, earlier)
    def _(d):
        sent(kv.at[d, core], kf_s.at[d], kf_r.at[d])
        sent(dkv.at[d, 1 - core], ds_s.at[d], ds_r.at[d])
        sent(dkv.at[d, core], da_s.at[d], da_r.at[d])

    for s in range(SUBS):

        @pl.loop(0, 8)
        def _(i):
            @pl.when(i != expert)
            def _():
                sent(packed.at[s, i], pa_s.at[s, i], pa_r.at[s, i])

            @pl.when(source_of(i) != c)
            def _():
                sent(unpacked.at[s, i], pr_s.at[s, i], pr_r.at[s, i])

        @pl.loop(0, EXPERTS)
        def _(i):
            got(ret.at[s, i], pr_s.at[s, i], pr_r.at[s, i])

    rows = ret[...].reshape(SUBS * SPREAD, COLS)
    total = jnp.zeros((CT, COLS), F32)
    for k in range(2):
        weight = jnp.transpose(jnp.broadcast_to(rw_ref[k : k + 1, :], (CT, CT)))[:, :1]
        total = total + weight * dot(pick[k].astype(BF16), rows, TN)
    dm_ref[...] = total.astype(BF16)


def finish(*refs):
    for src, dst in zip(refs[:4], refs[4:]):
        dst[...] = src[...]


def per_device(
    queries, key_rows, value_rows, attn_out, grad_out, segments, grad_moe_out,
    expert_ids, route_weights, saved_gate, saved_up, w_gate, w_up, w_down,
):
    order = np.zeros((4, SUBS, 4, THIRD, 4, 4, CAP), np.float32)
    for part in range(4):
        for at in range(4):
            diff = ((0, 1, 1, 2), (2, 3, 0, 3))[part // 2][at]
            for s in range(SUBS):
                for i in range(THIRD):
                    order[part, s, at, i, diff, 2 * (at // 2) + part % 2, THIRD * s + i] = 1
    order = jnp.asarray(order.reshape(4 * SET, 4 * SET), BF16)
    vmem = pl.BlockSpec(memory_space=pltpu.VMEM)
    hbm = pl.BlockSpec(memory_space=pl.ANY)
    dma = pltpu.SemaphoreType.DMA
    slots = WINDOW + 1
    shapes = [
        jax.ShapeDtypeStruct((CT, HEADS * HEAD), BF16),
        jax.ShapeDtypeStruct((CT, HEAD), BF16),
        jax.ShapeDtypeStruct((CT, HEAD), BF16),
        jax.ShapeDtypeStruct((CT, COLS), BF16),
    ]
    scratch = [
        pltpu.VMEM((slots, 2, CT, 2 * HEAD), BF16),
        pltpu.VMEM((slots, 2 * CT, HEADS * CT), F32),
        pltpu.VMEM((HEADS * CT, HEAD), BF16),
        pltpu.VMEM((HEADS * CT, HEAD), BF16),
        pltpu.VMEM((slots, 2, CT, 2 * HEAD), BF16),
        pltpu.VMEM((slots, CT, 2 * HEAD), BF16),
        pltpu.VMEM((slots, CT, 2 * HEAD), BF16),
        pltpu.VMEM((CT, COLS), BF16),
        pltpu.VMEM((SUBS, EXPERTS, TILE, COLS), BF16),
        pltpu.VMEM((SUBS, 8, TILE, COLS), BF16),
        pltpu.VMEM((2, BLOCK, WIDE), BF16),
        pltpu.VMEM((2, 4, SET, HID), BF16),
        pltpu.VMEM((2, 4, SET, HID), BF16),
        pltpu.VMEM((4 * SET, 4 * SET), BF16),
        pltpu.VMEM((2, 2, SUBS, 2, SUB // 2, HID), BF16),
        pltpu.VMEM((2, 2, SUBS, 2, SUB // 2, HID), BF16),
        pltpu.VMEM((2, SUBS, 2, SUB // 2, HID), BF16),
        pltpu.VMEM((2, SUBS, 2, SUB // 2, HID), BF16),
        pltpu.VMEM((2, WIDE, HID), BF16),
        pltpu.VMEM((2, WIDE, HID), BF16),
        pltpu.VMEM((2, HID, WIDE), BF16),
        pltpu.VMEM((2, BLOCK, WIDE), BF16),
        pltpu.VMEM((SUBS, 2, 4, SUB, COLS), BF16),
        pltpu.VMEM((SUBS, 2, 2, 3, SUB, COLS), BF16),
        pltpu.VMEM((SUBS, SUB, COLS), BF16),
        pltpu.VMEM((SUBS, SUB, COLS), BF16),
        pltpu.VMEM((SUBS, 8, TILE, COLS), BF16),
        pltpu.VMEM((SUBS, EXPERTS, TILE, COLS), BF16),
        dma((21,)),
    ]
    for shape in (
        (slots,), (slots,), (slots,), (slots,),
        (SUBS, 8),
        (SUBS,), (SUBS, 2, 2, 4), (SUBS, 2, 4), (3,),
        (2, 2), (SUBS, 2, 4), (SUBS, 2, 2, 4), (SUBS,),
        (SUBS, 8),
    ):
        scratch += [dma(shape), dma(shape)]
    results = pl.pallas_call(
        kernel,
        out_shape=shapes,
        in_specs=[vmem] * 6 + [hbm] + [vmem] * 2 + [hbm] * 6,
        out_specs=[vmem] * 4,
        scratch_shapes=scratch,
        compiler_params=pltpu.CompilerParams(
            collective_id=0, has_side_effects=True, vmem_limit_bytes=60 * 2**20
        ),
        cost_estimate=pl.CostEstimate(
            flops=13 * 10**9, bytes_accessed=12 * 10**6, transcendentals=2 * 10**6
        ),
    )(
        queries, key_rows, value_rows, attn_out, grad_out,
        segments.reshape(N_CTX, CT), grad_moe_out, expert_ids.T, route_weights.T,
        saved_gate.reshape(8, SET, HID), saved_up.reshape(8, SET, HID), order,
        w_gate, w_up, w_down,
    )
    return pl.pallas_call(
        finish, out_shape=shapes, in_specs=[vmem] * 4, out_specs=[vmem] * 4
    )(*results)


def solution(mesh):
    in_specs = (
        P("ctx", "tp"), P("ctx", "tp"), P("ctx", "tp"), P("ctx", "tp"), P("ctx", "tp"),
        P(), P("ctx", None), P("ctx", None), P("ctx", None),
        P("ctx", "tp"), P("ctx", "tp"),
        P(None, ("ctx", "tp")), P(None, ("ctx", "tp")), P(("ctx", "tp"), None),
    )
    out_specs = (P("ctx", "tp"), P("ctx", "tp"), P("ctx", "tp"), P("ctx", "tp"))
    return jax.shard_map(
        per_device, mesh=mesh, in_specs=in_specs, out_specs=out_specs, check_vma=False
    )
```

```python
import jax
import jax.numpy as jnp
import numpy as np
from jax import lax
from jax.experimental import pallas as pl
from jax.experimental.pallas import tpu as pltpu
from jax.sharding import PartitionSpec as P

EXPERTS = 8
HEAD = 128
CAP = 36
THIRD = 12
TILE = 16
SPREAD = 8 * TILE
CT = 128
N_CTX = 32
HEADS = 3
WINDOW = 10
CHIPS = 16
SUBS = 3
SUB = 96
Y_LAST = (2,)
BLOCK = 288
SET = 144
COLS = 384
HALF = 1536
WIDE = 3072
HID = 512
MESH = pl.DeviceIdType.MESH
F32 = jnp.float32
BF16 = jnp.bfloat16
NT = (((1,), (1,)), ((), ()))
NN = (((1,), (0,)), ((), ()))
TN = (((0,), (0,)), ((), ()))


def dot(a, b, dims):
    return lax.dot_general(a, b, dims, preferred_element_type=F32)


def kernel(
    q_ref, k_ref, v_ref, ao_ref, go_ref, seg_ref, gm_ref, ids_ref, rw_ref,
    sg_ref, su_ref, perm_ref, wg_ref, wu_ref, wd_ref,
    dq_ref, dk_ref, dv_ref, dm_ref,
    kv, st, q3, g3, dkv, dks, dacc,
    gm, packed, arrive, arr, sgr, sur, perm, sg, su, sgx, sux, wg, wu, wd,
    part, b1, b2, b3s, b3, unpacked, ret,
    ld_sem, kv_s, kv_r, kf_s, kf_r, ds_s, ds_r, da_s, da_r,
    pa_s, pa_r, g1_s, g1_r, g2_s, g2_r, g3_s, g3_r, w_s, w_r,
    x_s, x_r, r1_s, r1_r, r2_s, r2_r, r3_s, r3_r, pr_s, pr_r,
):
    c = lax.axis_index("ctx")
    u = lax.axis_index("tp")
    core = c % 2
    chip = c // 2
    zp = chip % 2
    xh = u // 4
    y = u % 4
    quarter = c % 4
    sibling = (c + 1 - 2 * core, u)
    first = (c + core * (2 - 4 * zp), u + (1 - core) * (4 - 8 * xh))
    last = (c + (1 - core) * (2 - 4 * zp), u + core * (4 - 8 * xh))

    def along_y(dy):
        return (c, xh * 4 + (y + dy) % 4)

    def send(src, dst, ss, rs, to):
        pltpu.make_async_remote_copy(
            src_ref=src, dst_ref=dst, send_sem=ss, recv_sem=rs,
            device_id=to, device_id_type=MESH,
        ).start()

    def got(dst, ss, rs):
        pltpu.make_async_remote_copy(
            src_ref=dst, dst_ref=dst, send_sem=ss, recv_sem=rs,
            device_id=sibling, device_id_type=MESH,
        ).wait_recv()

    def sent(src, ss, rs):
        pltpu.make_async_remote_copy(
            src_ref=src, dst_ref=src, send_sem=ss, recv_sem=rs,
            device_id=sibling, device_id_type=MESH,
        ).wait_send()

    barrier = pltpu.get_barrier_semaphore()

    for i in range(1, N_CTX):
        pl.semaphore_signal(
            barrier, inc=1, device_id=((c + i) % N_CTX, u), device_id_type=MESH
        )
    for dy in (1, 2, 3):
        pl.semaphore_signal(barrier, inc=1, device_id=along_y(dy), device_id_type=MESH)
    pl.semaphore_signal(
        barrier, inc=1, device_id=(c, u + 4 - 8 * xh), device_id_type=MESH
    )

    own_cols = pl.ds(pl.multiple_of(u * COLS, 128), COLS)
    expert = c // 4
    rank_pair = expert % 4
    loads = [(gm_ref.at[:, own_cols], gm), (perm_ref, perm)]
    for x in (0, 1):
        for diff in range(4):
            group = 4 * x + (rank_pair + 4 - diff) % 4
            loads += [(sg_ref.at[group], sgr.at[x, diff]), (su_ref.at[group], sur.at[x, diff])]
    weights = [(wd_ref, wd.at[core]), (wg_ref, wg.at[core]), (wu_ref, wu.at[core])]
    loads += weights

    def load(i):
        return pltpu.make_async_copy(loads[i][0], loads[i][1], ld_sem.at[i])

    for i in range(len(loads)):
        load(i).start()

    ids = ids_ref[...]
    expert_row = lax.broadcasted_iota(jnp.int32, (EXPERTS, CT), 0)
    hot = [(ids[k : k + 1, :] == expert_row).astype(F32) for k in range(2)]
    before = (
        lax.broadcasted_iota(jnp.int32, (CT, CT), 0) < lax.broadcasted_iota(jnp.int32, (CT, CT), 1)
    ).astype(BF16)
    rank = dot((hot[0] + hot[1]).astype(BF16), before, NN)
    third = (rank >= THIRD).astype(F32) + (rank >= 2 * THIRD).astype(F32)
    place = rank + (SPREAD - THIRD) * third + (TILE * expert_row).astype(F32)
    slot_row = lax.broadcasted_iota(jnp.int32, (SUBS * SPREAD, CT), 0)
    pick = []
    for k in range(2):
        slot = jnp.sum(hot[k] * place, axis=0, keepdims=True).astype(jnp.int32)
        pick.append((slot_row == slot).astype(F32))
    selector = (pick[0] + pick[1]).astype(BF16)
    load(0).wait()
    packed[...] = dot(selector, gm[...], NN).astype(BF16).reshape(SUBS, EXPERTS, TILE, COLS)
    kv[0, core, :, :HEAD] = k_ref[...]
    kv[0, core, :, HEAD:] = v_ref[...]

    pl.semaphore_wait(barrier, N_CTX - 1 + 4)

    own_x = c // 16
    own_pair = (chip % 8) // 2
    for s in range(SUBS):

        @pl.loop(0, EXPERTS)
        def _(e):
            diff = (e % 4 - own_pair + 4) % 4
            to_z = (1 - zp) * (diff // 2) + zp * (((diff + 1) // 2 + 1) % 2)
            slot = 4 * own_x + (1 - zp) * (diff % 2) + zp * (2 + diff // 2)
            to = ((e // 4) * 8 + 2 * (e % 4) + to_z) * 2 + core

            @pl.when(e == expert)
            def _():
                pltpu.make_async_copy(
                    packed.at[s, e], arrive.at[s, slot], pa_r.at[s, slot]
                ).start()

            @pl.when(e != expert)
            def _():
                send(
                    packed.at[s, e], arrive.at[s, slot],
                    pa_s.at[s, e], pa_r.at[s, slot], (to, u),
                )

    later = jnp.minimum(WINDOW, CHIPS - 1 - chip) + 1
    earlier = jnp.minimum(WINDOW, chip) + 1

    send(kv.at[0, core], kv.at[0, core], kf_s.at[0], kf_r.at[0], sibling)

    @pl.loop(1, later)
    def _(d):
        send(kv.at[0, core], kv.at[d, core], kv_s.at[d], kv_r.at[d], (c + 2 * d, u))

    for i, (src, dst) in enumerate(weights):
        send(src, dst, w_s.at[i], w_r.at[i], sibling)

    q3[...] = jnp.concatenate([q_ref[:, h * HEAD : (h + 1) * HEAD] for h in range(HEADS)], axis=0)
    g3[...] = jnp.concatenate([go_ref[:, h * HEAD : (h + 1) * HEAD] for h in range(HEADS)], axis=0)
    a3 = jnp.concatenate([ao_ref[:, h * HEAD : (h + 1) * HEAD] for h in range(HEADS)], axis=0)
    row_dots = jnp.sum(
        jnp.transpose(g3[...].astype(F32) * a3.astype(F32)), axis=0, keepdims=True
    )
    segs = seg_ref[...]
    starts = [
        jnp.sum((segs < k).astype(F32)).astype(jnp.int32) for k in (1, 2)
    ]
    own_seg = seg_ref[pl.ds(c, 1), :]
    start = jnp.where(own_seg == 0, 0, jnp.where(own_seg == 1, starts[0], starts[1]))
    start = jnp.concatenate([start] * HEADS, axis=1)
    own_pos = c * CT + lax.broadcasted_iota(jnp.int32, (1, CT), 1)
    own_pos = jnp.concatenate([own_pos] * HEADS, axis=1)

    def order_saved():
        for i in range(1, 18):
            load(i).wait()
        for raw, ordered in ((sgr, sg), (sur, su)):
            for x in (0, 1):
                rows = dot(perm[...], raw[x].reshape(4 * SET, HID), NN).astype(BF16)
                ordered[:, :, :, x] = rows.reshape(2, 2, SUBS, SUB // 2, HID)
        for i, (src, dst) in enumerate(((sg, sgx), (su, sux))):
            for j in (0, 1):
                send(src.at[j, 1 - core], dst.at[j], x_s.at[i, j], x_r.at[i, j], sibling)

    def dense_map(shape, row_axis):
        rows = lax.broadcasted_iota(jnp.int32, shape, row_axis)
        slots = lax.broadcasted_iota(jnp.int32, shape, 1 - row_axis)
        group = sum((rows >= THIRD * i).astype(jnp.int32) for i in range(1, 8))
        return (slots == rows + (TILE - THIRD) * group).astype(BF16)

    def dense(s):
        @pl.loop(0, 8)
        def _(i):
            got(arrive.at[s, i], pa_s.at[s, i], pa_r.at[s, i])

        arr[zp, s * SUB : (s + 1) * SUB, own_cols] = dot(
            dense_map((SUB, SPREAD), 0), arrive[s].reshape(SPREAD, COLS), NN
        ).astype(BF16)

    def at_block(fr, lr):
        dz = lr * (1 - core) + fr * core
        dx = fr * (1 - core) + lr * core
        return zp + dz * (1 - 2 * zp), xh + dx * (1 - 2 * xh)

    def piece(ref, s, fr, lr, py):
        row, col = at_block(fr, lr)
        return ref.at[
            row, pl.ds(s * SUB, SUB), pl.ds(pl.multiple_of(col * HALF + py * COLS, 128), COLS)
        ]

    def y_at(dy):
        return (y + dy) % 4

    def to_last(s, fr, dy):
        mine = piece(arr, s, fr, 0, y_at(4 - dy))
        send(mine, mine, g3_s.at[s, fr, dy], g3_r.at[s, fr, dy], last)

    def to_y(s, fr, lr):
        mine = piece(arr, s, fr, lr, y)
        for dy in (1, 2, 3):
            send(mine, mine, g2_s.at[s, fr, lr, dy], g2_r.at[s, fr, lr, dy], along_y(dy))

    def from_y(s, fr, lr, dy):
        got(
            piece(arr, s, fr, lr, y_at(4 - dy)),
            g2_s.at[s, fr, lr, dy], g2_r.at[s, fr, lr, dy],
        )

    def from_last(s, fr, dy):
        got(piece(arr, s, fr, 1, y_at(4 - dy)), g3_s.at[s, fr, dy], g3_r.at[s, fr, dy])

    def gather_1(s):
        dense(s)
        mine = piece(arr, s, 0, 0, y)
        send(mine, mine, g1_s.at[s], g1_r.at[s], first)
        to_y(s, 0, 0)
        to_last(s, 0, 0)

    def gather_2(s):
        got(piece(arr, s, 1, 0, y), g1_s.at[s], g1_r.at[s])
        to_y(s, 1, 0)
        to_last(s, 1, 0)

    def gather_3(s):
        for fr in (0, 1):
            if s in Y_LAST:
                from_last(s, fr, 0)
                to_y(s, fr, 1)
            else:
                for dy in (1, 2, 3):
                    from_y(s, fr, 0, dy)
                    to_last(s, fr, dy)

    def gather_4(s):
        for fr in (0, 1):
            for lr in (0, 1) if s in Y_LAST else (1,):
                for dy in range(4):
                    if s not in Y_LAST:
                        from_last(s, fr, dy)
                    elif dy > 0:
                        from_y(s, fr, lr, dy)

    def wait_weights():
        for i in range(18, 21):
            load(i).wait()
        for i, (src, _) in enumerate(weights):
            got((wd, wg, wu)[i].at[1 - core], w_s.at[i], w_r.at[i])
        for i, dst in enumerate((sgx, sux)):
            for j in (0, 1):
                got(dst.at[j], x_s.at[i, j], x_r.at[i, j])

    def expert_rows(s):
        rows = pl.ds(s * SUB, SUB)
        grads = []
        for k, gate, up in (
            (core, sg[:, core, s], su[:, core, s]),
            (1 - core, sgx[:, s], sux[:, s]),
        ):
            hidden = dot(arr[:, rows, :].reshape(2 * SUB, WIDE), wd[k], NT)
            gate = gate.reshape(2 * SUB, HID).astype(F32)
            up = up.reshape(2 * SUB, HID).astype(F32)
            sig = jax.nn.sigmoid(gate)
            hs = hidden * sig
            grad_up = (hs * gate).astype(BF16)
            grad_gate = (hs * up * (1.0 + gate * (1.0 - sig))).astype(BF16)
            grads.append((k, grad_gate, grad_up))

        @pl.loop(0, WIDE // HID)
        def _(n):
            cols = pl.ds(pl.multiple_of(n * HID, HID), HID)
            out = sum(
                dot(grad_gate, wg[k, cols, :], NT) + dot(grad_up, wu[k, cols, :], NT)
                for k, grad_gate, grad_up in grads
            )
            part[:, rows, cols] = out.astype(BF16).reshape(2, SUB, HID)

    def part_at(s, fr, lr, py):
        row, col = at_block(fr, lr)
        cols = pl.ds(pl.multiple_of(col * HALF + py * COLS, 128), COLS)
        return part[row, pl.ds(s * SUB, SUB), cols].astype(F32)

    def half_to_last(s, fr, dy):
        mine = piece(part, s, fr, 1, y_at(dy))
        send(mine, b1.at[s, fr, dy], r1_s.at[s, fr, dy], r1_r.at[s, fr, dy], last)

    def half_to_y(s, fr, lr, dy):
        send(
            piece(part, s, fr, lr, y_at(dy)), b2.at[s, fr, lr, dy - 1],
            r2_s.at[s, fr, lr, dy], r2_r.at[s, fr, lr, dy], along_y(dy),
        )

    def add_last(s, fr, dy):
        got(b1.at[s, fr, dy], r1_s.at[s, fr, dy], r1_r.at[s, fr, dy])
        return b1[s, fr, dy].astype(F32)

    def add_y(s, fr, lr):
        total = part_at(s, fr, lr, y)
        for dy in (1, 2, 3):
            got(b2.at[s, fr, lr, dy - 1], r2_s.at[s, fr, lr, dy], r2_r.at[s, fr, lr, dy])
            total = total + b2[s, fr, lr, dy - 1].astype(F32)
        return total

    def return_1(s):
        if s in Y_LAST:
            for lr in (1, 0):
                for fr in (1, 0):
                    for dy in (1, 2, 3):
                        half_to_y(s, fr, lr, dy)
        else:
            for dy in (1, 2, 3, 0):
                for fr in (1, 0):
                    half_to_last(s, fr, dy)

    def return_2(s):
        for fr in (1, 0):
            if s in Y_LAST:
                mine = piece(part, s, fr, 1, y)
                mine[...] = add_y(s, fr, 1).astype(BF16)
                half_to_last(s, fr, 0)
            else:
                for dy in (1, 2, 3):
                    mine = piece(part, s, fr, 0, y_at(dy))
                    total = part_at(s, fr, 0, y_at(dy)) + add_last(s, fr, dy)
                    mine[...] = total.astype(BF16)
                    half_to_y(s, fr, 0, dy)

    def return_3(s):
        b3s[s] = (add_y(s, 1, 0) + add_last(s, 1, 0)).astype(BF16)
        send(b3s.at[s], b3.at[s], r3_s.at[s], r3_r.at[s], first)

    def return_4(s):
        total = add_y(s, 0, 0) + add_last(s, 0, 0)
        got(b3.at[s], r3_s.at[s], r3_r.at[s])
        rows = (total + b3[s].astype(F32)).astype(BF16)
        unpacked[s] = (
            dot(dense_map((SPREAD, SUB), 1), rows, NN).astype(BF16).reshape(8, TILE, COLS)
        )

        @pl.loop(0, 8)
        def _(i):
            to = source_of(i)

            @pl.when(to == c)
            def _():
                pltpu.make_async_copy(
                    unpacked.at[s, i], ret.at[s, expert], pr_r.at[s, expert]
                ).start()

            @pl.when(to != c)
            def _():
                send(
                    unpacked.at[s, i], ret.at[s, expert],
                    pr_s.at[s, i], pr_r.at[s, expert], (to, u),
                )

    def source_of(i):
        at = i % 4
        from_z = at // 2
        diff = (1 - zp) * (at - from_z) + zp * ((at + 2) * (1 - from_z) + 3 * from_z * (at % 2))
        return ((i // 4) * 8 + 2 * ((rank_pair + 4 - diff) % 4) + from_z) * 2 + core

    def keys_forward():
        @pl.loop(1, earlier)
        def _(d):
            mine = kv.at[d, core]
            got(mine, kv_s.at[d], kv_r.at[d])
            send(mine, mine, kf_s.at[d], kf_r.at[d], sibling)

    def keys_of(d):
        return kv[d, :, :, :HEAD].reshape(2 * CT, HEAD)

    def scores_pass():
        def step(d, top):
            got(kv.at[d, 1 - core], kf_s.at[d], kf_r.at[d])
            s = dot(keys_of(d), q3[...], NT) * (HEAD ** -0.5)
            pos = (chip - d) * 2 * CT + lax.broadcasted_iota(jnp.int32, (2 * CT, 1), 0)
            s = jnp.where((pos <= own_pos) & (pos >= start), s, -1e30)
            st[d] = s
            return jnp.maximum(top, jnp.max(s, axis=0, keepdims=True))

        top = lax.fori_loop(0, earlier, step, jnp.full((1, HEADS * CT), -1e30, F32))

        def step_2(d, total):
            p = jnp.exp(st[d] - top)
            st[d] = p
            return total + jnp.sum(p, axis=0, keepdims=True)

        total = lax.fori_loop(0, earlier, step_2, jnp.zeros((1, HEADS * CT), F32))
        return 1.0 / total

    def grads_pass(inverse):
        def step(d, dqt):
            probs = st[d] * inverse
            keys = keys_of(d)
            values = kv[d, :, :, HEAD:].reshape(2 * CT, HEAD)
            grad_probs = dot(values, g3[...], NT)
            grad_scores = (probs * (grad_probs - row_dots)).astype(BF16)
            dkv[d, :, :, :HEAD] = (
                (dot(grad_scores, q3[...], NN) * (HEAD ** -0.5)).astype(BF16).reshape(2, CT, HEAD)
            )
            dkv[d, :, :, HEAD:] = (
                dot(probs.astype(BF16), g3[...], NN).astype(BF16).reshape(2, CT, HEAD)
            )
            send(dkv.at[d, 1 - core], dks.at[d], ds_s.at[d], ds_r.at[d], sibling)
            return dqt + dot(keys, grad_scores, TN)

        dqt = lax.fori_loop(0, earlier, step, jnp.zeros((HEAD, HEADS * CT), F32))
        dq = jnp.transpose(dqt * (HEAD ** -0.5)).astype(BF16)
        for h in range(HEADS):
            dq_ref[:, h * HEAD : (h + 1) * HEAD] = dq[h * CT : (h + 1) * CT, :]

    def keys_return():
        @pl.loop(0, earlier)
        def _(d):
            got(dks.at[d], ds_s.at[d], ds_r.at[d])
            dkv[d, core] = (dkv[d, core].astype(F32) + dks[d].astype(F32)).astype(BF16)

            @pl.when(d > 0)
            def _():
                send(dkv.at[d, core], dacc.at[d], da_s.at[d], da_r.at[d], (c - 2 * d, u))

    def keys_finish():
        def step(d, total):
            got(dacc.at[d], da_s.at[d], da_r.at[d])
            return total + dacc[d].astype(F32)

        total = lax.fori_loop(1, later, step, dkv[0, core].astype(F32))
        dk_ref[...] = total[:, :HEAD].astype(BF16)
        dv_ref[...] = total[:, HEAD:].astype(BF16)

    order_saved()
    gather_1(0)
    gather_1(1)
    gather_2(0)
    gather_1(2)
    gather_2(1)
    gather_2(2)
    gather_3(0)
    keys_forward()
    gather_3(1)
    gather_3(2)
    gather_4(0)
    wait_weights()
    expert_rows(0)
    return_1(0)
    gather_4(1)
    expert_rows(1)
    return_1(1)
    inverse = scores_pass()
    return_2(0)
    gather_4(2)
    expert_rows(2)
    return_1(2)
    grads_pass(inverse)
    return_2(1)
    return_3(0)
    return_2(2)
    keys_return()
    return_4(0)
    return_3(1)
    return_4(1)
    return_3(2)
    return_4(2)
    keys_finish()

    for s in range(SUBS):
        sent(b3s.at[s], g1_s.at[s], g1_r.at[s])
        sent(b3s.at[s], r3_s.at[s], r3_r.at[s])
        for fr in (0, 1):
            for dy in range(1 if s in Y_LAST else 4):
                sent(b3s.at[s], g3_s.at[s, fr, dy], g3_r.at[s, fr, dy])
                sent(b3s.at[s], r1_s.at[s, fr, dy], r1_r.at[s, fr, dy])
            for lr in (0, 1) if s in Y_LAST else (0,):
                for dy in (1, 2, 3):
                    sent(b3s.at[s], g2_s.at[s, fr, lr, dy], g2_r.at[s, fr, lr, dy])
                    sent(b3s.at[s], r2_s.at[s, fr, lr, dy], r2_r.at[s, fr, lr, dy])
    for i, (_, dst) in enumerate(weights):
        sent(dst, w_s.at[i], w_r.at[i])
    for i, src in enumerate((sgx, sux)):
        for j in (0, 1):
            sent(src.at[j], x_s.at[i, j], x_r.at[i, j])
    sent(kv.at[0, core], kf_s.at[0], kf_r.at[0])
    sent(dkv.at[0, core], ds_s.at[0], ds_r.at[0])

    @pl.loop(1, later)
    def _(d):
        sent(kv.at[0, core], kv_s.at[d], kv_r.at[d])

    @pl.loop(1, earlier)
    def _(d):
        sent(kv.at[d, core], kf_s.at[d], kf_r.at[d])
        sent(dkv.at[d, 1 - core], ds_s.at[d], ds_r.at[d])
        sent(dkv.at[d, core], da_s.at[d], da_r.at[d])

    for s in range(SUBS):

        @pl.loop(0, 8)
        def _(i):
            @pl.when(i != expert)
            def _():
                sent(packed.at[s, i], pa_s.at[s, i], pa_r.at[s, i])

            @pl.when(source_of(i) != c)
            def _():
                sent(unpacked.at[s, i], pr_s.at[s, i], pr_r.at[s, i])

        @pl.loop(0, EXPERTS)
        def _(i):
            got(ret.at[s, i], pr_s.at[s, i], pr_r.at[s, i])

    rows = ret[...].reshape(SUBS * SPREAD, COLS)
    total = jnp.zeros((CT, COLS), F32)
    for k in range(2):
        weight = jnp.transpose(jnp.broadcast_to(rw_ref[k : k + 1, :], (CT, CT)))[:, :1]
        total = total + weight * dot(pick[k].astype(BF16), rows, TN)
    dm_ref[...] = total.astype(BF16)


def finish(*refs):
    for src, dst in zip(refs[:4], refs[4:]):
        dst[...] = src[...]


def per_device(
    queries, key_rows, value_rows, attn_out, grad_out, segments, grad_moe_out,
    expert_ids, route_weights, saved_gate, saved_up, w_gate, w_up, w_down,
):
    order = np.zeros((4, SUBS, 4, THIRD, 4, 4, CAP), np.float32)
    for part in range(4):
        for at in range(4):
            diff = ((0, 1, 1, 2), (2, 3, 0, 3))[part // 2][at]
            for s in range(SUBS):
                for i in range(THIRD):
                    order[part, s, at, i, diff, 2 * (at // 2) + part % 2, THIRD * s + i] = 1
    order = jnp.asarray(order.reshape(4 * SET, 4 * SET), BF16)
    vmem = pl.BlockSpec(memory_space=pltpu.VMEM)
    hbm = pl.BlockSpec(memory_space=pl.ANY)
    dma = pltpu.SemaphoreType.DMA
    slots = WINDOW + 1
    shapes = [
        jax.ShapeDtypeStruct((CT, HEADS * HEAD), BF16),
        jax.ShapeDtypeStruct((CT, HEAD), BF16),
        jax.ShapeDtypeStruct((CT, HEAD), BF16),
        jax.ShapeDtypeStruct((CT, COLS), BF16),
    ]
    scratch = [
        pltpu.VMEM((slots, 2, CT, 2 * HEAD), BF16),
        pltpu.VMEM((slots, 2 * CT, HEADS * CT), F32),
        pltpu.VMEM((HEADS * CT, HEAD), BF16),
        pltpu.VMEM((HEADS * CT, HEAD), BF16),
        pltpu.VMEM((slots, 2, CT, 2 * HEAD), BF16),
        pltpu.VMEM((slots, CT, 2 * HEAD), BF16),
        pltpu.VMEM((slots, CT, 2 * HEAD), BF16),
        pltpu.VMEM((CT, COLS), BF16),
        pltpu.VMEM((SUBS, EXPERTS, TILE, COLS), BF16),
        pltpu.VMEM((SUBS, 8, TILE, COLS), BF16),
        pltpu.VMEM((2, BLOCK, WIDE), BF16),
        pltpu.VMEM((2, 4, SET, HID), BF16),
        pltpu.VMEM((2, 4, SET, HID), BF16),
        pltpu.VMEM((4 * SET, 4 * SET), BF16),
        pltpu.VMEM((2, 2, SUBS, 2, SUB // 2, HID), BF16),
        pltpu.VMEM((2, 2, SUBS, 2, SUB // 2, HID), BF16),
        pltpu.VMEM((2, SUBS, 2, SUB // 2, HID), BF16),
        pltpu.VMEM((2, SUBS, 2, SUB // 2, HID), BF16),
        pltpu.VMEM((2, WIDE, HID), BF16),
        pltpu.VMEM((2, WIDE, HID), BF16),
        pltpu.VMEM((2, HID, WIDE), BF16),
        pltpu.VMEM((2, BLOCK, WIDE), BF16),
        pltpu.VMEM((SUBS, 2, 4, SUB, COLS), BF16),
        pltpu.VMEM((SUBS, 2, 2, 3, SUB, COLS), BF16),
        pltpu.VMEM((SUBS, SUB, COLS), BF16),
        pltpu.VMEM((SUBS, SUB, COLS), BF16),
        pltpu.VMEM((SUBS, 8, TILE, COLS), BF16),
        pltpu.VMEM((SUBS, EXPERTS, TILE, COLS), BF16),
        dma((21,)),
    ]
    for shape in (
        (slots,), (slots,), (slots,), (slots,),
        (SUBS, 8),
        (SUBS,), (SUBS, 2, 2, 4), (SUBS, 2, 4), (3,),
        (2, 2), (SUBS, 2, 4), (SUBS, 2, 2, 4), (SUBS,),
        (SUBS, 8),
    ):
        scratch += [dma(shape), dma(shape)]
    results = pl.pallas_call(
        kernel,
        out_shape=shapes,
        in_specs=[vmem] * 6 + [hbm] + [vmem] * 2 + [hbm] * 6,
        out_specs=[vmem] * 4,
        scratch_shapes=scratch,
        compiler_params=pltpu.CompilerParams(
            collective_id=0, has_side_effects=True, vmem_limit_bytes=60 * 2**20
        ),
        cost_estimate=pl.CostEstimate(
            flops=13 * 10**9, bytes_accessed=12 * 10**6, transcendentals=2 * 10**6
        ),
    )(
        queries, key_rows, value_rows, attn_out, grad_out,
        segments.reshape(N_CTX, CT), grad_moe_out, expert_ids.T, route_weights.T,
        saved_gate.reshape(8, SET, HID), saved_up.reshape(8, SET, HID), order,
        w_gate, w_up, w_down,
    )
    return pl.pallas_call(
        finish, out_shape=shapes, in_specs=[vmem] * 4, out_specs=[vmem] * 4
    )(*results)


def solution(mesh):
    in_specs = (
        P("ctx", "tp"), P("ctx", "tp"), P("ctx", "tp"), P("ctx", "tp"), P("ctx", "tp"),
        P(), P("ctx", None), P("ctx", None), P("ctx", None),
        P("ctx", "tp"), P("ctx", "tp"),
        P(None, ("ctx", "tp")), P(None, ("ctx", "tp")), P(("ctx", "tp"), None),
    )
    out_specs = (P("ctx", "tp"), P("ctx", "tp"), P("ctx", "tp"), P("ctx", "tp"))
    return jax.shard_map(
        per_device, mesh=mesh, in_specs=in_specs, out_specs=out_specs, check_vma=False
    )
```
